32 devices in a mesh: blk: 8 (over z, y), head: 4 (over x, core).
Axes of the slice: x: 2, y: 2, z: 4, core: 2. Of those that a mesh axis runs over, the one named last changes fastest.
Arguments:
- query_rows: bfloat16 [8192, 1024], P(('blk', 'head')), may hold values from -8 to 8
- key_rows: bfloat16 [8192, 1024], P(('blk', 'head')), may hold values from -8 to 8
- value_rows: bfloat16 [8192, 1024], P(('blk', 'head')), may hold values from -6 to 6
- out_grad: bfloat16 [8192, 1024], P(('blk', 'head')), may hold values from -6 to 6
- expander_device: int32 [64, 4], P('blk'), may hold values from 0 to 7, all different within a row; in each aligned block of 8 rows (0 to 7, 8 to 15, ...) at most 8 rows name the same one
- expander_block: int32 [64, 4], P('blk'), may hold values from 0 to 7
- local_offset: int32 [64, 11], P('blk'), may hold values from -4 to 4
- live_count: int32 [64], P('blk'), may hold values from 3 to 4
- drop_seed: int32 [16, 64, 16], P('head', 'blk'), may hold values from 0 to 1048575
Outputs:
- attended: bfloat16 [8192, 1024], P(('blk', 'head'))
- query_grad: bfloat16 [8192, 1024], P(('blk', 'head'))
- key_grad: bfloat16 [8192, 1024], P(('blk', 'head'))
- value_grad: bfloat16 [8192, 1024], P(('blk', 'head'))
The draws below stay inside these ranges and needn't reach their ends.
Inputs may be any that keep to these rules, and one draw needn't show every extreme that they name: `expander_device`: each row names 4 different devices. Among the rows of one device (aligned blocks of 8 rows), no device is named by more than 8 rows, and in every draw some device is named exactly 8 times by one device's rows.
All inputs are finite; a program needn't handle non-finite values.
Results may differ from the reference program's by a relative error of at most 0.012.
Values may be sent and summed in bfloat16 or wider, within the bound.
A program may use at most 128 MiB of HBM per device.

```python
import math
import jax
import jax.numpy as jnp
import numpy as np
from jax import lax

H = 16
DH = 64
BS = 128
QB_DEV = 8
L = 11
E = 4
W = 4
NB = 16
PEERS = 8
CAP = 8
BLOCKS = 64
NODES = 8192
HW = 1024


def drawn_pair(key):
    grid_shape = (BLOCKS, BS, H * DH)
    query_seed = jax.random.fold_in(key, 101)
    key_seed = jax.random.fold_in(key, 102)
    query_gain_seed = jax.random.fold_in(key, 103)
    key_gain_seed = jax.random.fold_in(key, 104)
    query_base = jnp.clip(jax.random.normal(query_seed, grid_shape, jnp.float32), -4.0, 4.0)
    key_base = jnp.clip(jax.random.normal(key_seed, grid_shape, jnp.float32), -4.0, 4.0)
    query_gain = jnp.exp(jax.random.uniform(query_gain_seed, (BLOCKS, BS, 1), jnp.float32, -0.69, 0.69))
    key_gain = jnp.exp(jax.random.uniform(key_gain_seed, (BLOCKS, BS, 1), jnp.float32, -0.69, 0.69))
    query_base = query_base * query_gain
    key_base = key_base * key_gain
    return (query_base.reshape(NODES, H * DH), key_base.reshape(NODES, H * DH))


def draw_query_rows(key, part):
    return drawn_pair(key)[0].astype(jnp.bfloat16)


def draw_key_rows(key, part):
    return drawn_pair(key)[1].astype(jnp.bfloat16)


def with_ends(entries, rng, smallest, high):
    longest = entries.shape.index(max(entries.shape))
    spots = []
    for shift in (0, 1):
        where = [jax.random.randint(jax.random.fold_in(rng, axis), (), 0, length) for axis, length in enumerate(entries.shape)]
        where[longest] = (where[longest] + shift) % entries.shape[longest]
        spots.append(tuple(where))
    return entries.at[spots[0]].set(smallest).at[spots[1]].set(high)


def level_of(key, dims, pieces, least, high):
    loudness = 1.0
    for axis_at, parts in pieces:
        draws = jax.random.uniform(jax.random.fold_in(jax.random.fold_in(key, 6), axis_at), (parts,), jnp.float32, least / len(pieces), high / len(pieces))
        loudness = loudness * jnp.repeat(jnp.exp(draws), dims[axis_at] // parts).reshape((-1,) + (1,) * (len(dims) - 1 - axis_at))
    return loudness


def shared_out(key, own, number, rows, count, top, reach, lean):
    ranking = jax.random.permutation(key, count)
    crowded, usual = shares(count, rows * top, reach, lean, True), shares(count, rows * top, reach, lean, False)
    places = jnp.arange(count)

    def named(sizes, turn):
        used = int((sizes > 0).sum())
        fixed = max(1, used // 4)
        shifted = fixed + (places - fixed + turn * (used - fixed)) % max(1, count - fixed)
        return jnp.zeros((count,), jnp.int32).at[ranking[jnp.where(places < fixed, places, shifted)]].set(jnp.asarray(sizes, jnp.int32))

    sizes = jnp.where(number % 4 == 0, named(crowded, number // 4), named(usual, number - number // 4 - 1))
    mixed = jax.random.permutation(jax.random.fold_in(own, 3), count)
    giver, taker = mixed[0:count // 2 * 2:2], mixed[1:count // 2 * 2:2]
    margin = jnp.minimum(sizes[giver] - 1, reach - sizes[taker]) // 2
    margin = jnp.where((giver == ranking[0]) | (taker == ranking[0]) | (sizes[taker] == 0), 0, jnp.maximum(margin, 0))
    shifted = jax.random.randint(jax.random.fold_in(own, 4), (count // 2,), 0, 1 << 20) % (margin + 1)
    sizes = sizes.at[giver].add(-shifted).at[taker].add(shifted)
    members = jnp.searchsorted(jnp.cumsum(sizes), jnp.arange(rows * top), side="right").astype(jnp.int32)
    listing = members.reshape(top, rows).T
    listing = listing[jax.random.permutation(jax.random.fold_in(own, 1), rows)]
    turn = jax.random.randint(jax.random.fold_in(own, 2), (rows, 1), 0, top)
    return jnp.take_along_axis(listing, (jnp.arange(top)[None, :] + turn) % top, axis=1)


def shares(number_of, total, most, slope, full):
    weights = [(1 << 20) // math.isqrt(rank ** slope) + 1 for rank in range(1, number_of + 1)]
    largest = most if full else min(most, max(-(-total // number_of), total * weights[0] // sum(weights)))
    least = 1 if total - largest >= number_of - 1 else 0
    given, spare = [largest] + [least] * (number_of - 1), total - largest - least * (number_of - 1)
    while spare > 0:
        movable = [i for i in range(1, number_of) if given[i] < largest] or [i for i in range(1, number_of) if given[i] < most]
        whole, left = sum([weights[i] for i in movable]), spare
        for i in movable:
            more = min(most - given[i], max(1, left * weights[i] // whole), spare)
            given[i] = given[i] + more
            spare = spare - more
    return np.array(given)


def bell_draw(key, dims, spread, limit, pieces=(), kind=jnp.bfloat16):
    gain = level_of(key, dims, pieces, -0.22, 0.18) if pieces else 1.0
    result = jax.random.normal(key, dims, jnp.float32) * spread * gain
    return jnp.minimum(jnp.maximum(result, -limit), limit).astype(kind)


def setup_inputs(seed: int = 0) -> dict:
    seeds = jax.random.split(jax.random.key(seed), 10)
    query_rows = draw_query_rows(jax.random.fold_in(seeds[9], 71), 0)
    key_rows = draw_key_rows(jax.random.fold_in(seeds[9], 71), 0)
    value_rows = bell_draw(seeds[2], (NODES, HW), 1.0, 6.0, ((0, 32),))
    out_grad = bell_draw(seeds[3], (NODES, HW), 1.0, 6.0, ((0, 32),))
    expander_device_keys = jax.random.split(jax.random.fold_in(seeds[4], 1), BLOCKS // QB_DEV)
    expander_device_turns = jax.random.permutation(jax.random.fold_in(seeds[4], 3), BLOCKS // QB_DEV)
    expander_device = jax.vmap(lambda own, number: shared_out(jax.random.fold_in(seeds[4], 2), own, number, QB_DEV, PEERS, E, CAP, 2))(expander_device_keys, expander_device_turns).reshape((BLOCKS, E))
    expander_block = with_ends(jax.random.randint(seeds[5], (BLOCKS, E), 0, QB_DEV), jax.random.fold_in(seeds[5], 1), 0, QB_DEV - 1).astype(jnp.int32)
    local_offset = with_ends(jax.random.randint(seeds[6], (BLOCKS, L), 0 - W, W + 1), jax.random.fold_in(seeds[6], 1), 0 - W, W).astype(jnp.int32)
    live_count = with_ends(jax.random.randint(seeds[7], (BLOCKS,), 3, E + 1), jax.random.fold_in(seeds[7], 1), 3, E).astype(jnp.int32)
    drop_seed = with_ends(jax.random.randint(seeds[8], (H, BLOCKS, NB), 0, 1048576), jax.random.fold_in(seeds[8], 1), 0, 1048575).astype(jnp.int32)
    return {"query_rows": query_rows, "key_rows": key_rows, "value_rows": value_rows, "out_grad": out_grad, "expander_device": expander_device, "expander_block": expander_block, "local_offset": local_offset, "live_count": live_count, "drop_seed": drop_seed}


KEEP_LEVEL = 102
KEEP_GAIN = 1024.0 / 922.0
MASKED = -1.0e30


def logical_right(value, amount):
    return lax.shift_right_logical(value, jnp.full(value.shape, amount, jnp.int32))


def keep_weights(seed_row, block_size):
    row_index = jnp.arange(block_size, dtype=jnp.int32)[:, None, None]
    col_index = jnp.arange(block_size, dtype=jnp.int32)[None, None, :]
    offset = (row_index * block_size + col_index).astype(jnp.int32)
    hashed = (seed_row[:, None, :, None] * 40503 + offset[None]).astype(jnp.int32)
    hashed = hashed ^ logical_right(hashed, 15)
    hashed = (hashed * 739982445).astype(jnp.int32)
    hashed = hashed ^ logical_right(hashed, 12)
    hashed = (hashed * 695872825).astype(jnp.int32)
    hashed = hashed ^ logical_right(hashed, 15)
    keep_scale = jnp.where((hashed & 1023) >= KEEP_LEVEL, KEEP_GAIN, 0.0).astype(jnp.float32)
    return keep_scale.reshape(seed_row.shape[0], block_size, -1)


def rounded(value):
    return lax.optimization_barrier(value.astype(jnp.bfloat16)).astype(jnp.float32)


def block_terms(query_block, key_block, value_block, grad_block, live_keys, keep_scale, score_scale):
    query_wide = query_block.astype(jnp.float32)
    key_wide = key_block.astype(jnp.float32)
    value_wide = value_block.astype(jnp.float32)
    grad_wide = grad_block.astype(jnp.float32)
    scores = jnp.einsum("qhd,khd->hqk", query_wide, key_wide) * score_scale
    scores = jnp.where(live_keys[None, None, :], scores, MASKED)
    largest = jnp.max(scores, axis=-1, keepdims=True)
    expterm = jnp.exp(scores - largest)
    attention = expterm / jnp.sum(expterm, axis=-1, keepdims=True)
    dropped_wide = rounded(attention * keep_scale)
    attended_full = jnp.einsum("hqk,khd->qhd", dropped_wide, value_wide)
    row_delta = jnp.einsum("qhd,qhd->hq", grad_wide, attended_full)
    drop_grad = jnp.einsum("qhd,khd->hqk", grad_wide, value_wide)
    score_wide = rounded(attention * (drop_grad * keep_scale - row_delta[:, :, None]) * score_scale)
    query_grad = jnp.einsum("hqk,khd->qhd", score_wide, key_wide).astype(jnp.bfloat16)
    key_part = jnp.einsum("hqk,qhd->khd", score_wide, query_wide)
    value_part = jnp.einsum("hqk,qhd->khd", dropped_wide, grad_wide)
    return attended_full.astype(jnp.bfloat16), query_grad, key_part, value_part


def reference(query_rows, key_rows, value_rows, out_grad, expander_device, expander_block, local_offset, live_count, drop_seed):
    score_scale = DH ** -0.5
    slot_count = 1 + L + E
    block_ids = jnp.arange(BLOCKS, dtype=jnp.int32)[:, None]
    near_ids = ((block_ids + local_offset) % BLOCKS).astype(jnp.int32)
    far_ids = (expander_device * QB_DEV + expander_block).astype(jnp.int32)
    slot_blocks = jnp.concatenate([block_ids, near_ids, far_ids], axis=1).astype(jnp.int32)
    slot_index = jnp.arange(slot_count, dtype=jnp.int32)[None, :]
    live_slots = (slot_index <= L) | (slot_index - 1 - L < live_count[:, None])
    far_slots = (jnp.arange(slot_count, dtype=jnp.int32) > L)[:, None, None, None]
    grid_shape = (BLOCKS, BS, H, DH)
    query_grid = query_rows.reshape(grid_shape)
    key_grid = key_rows.reshape(grid_shape)
    value_grid = value_rows.reshape(grid_shape)
    grad_grid = out_grad.reshape(grid_shape)
    seed_rows = jnp.transpose(drop_seed, (1, 0, 2))

    def block_step(running, inputs):
        key_total, value_total = running
        query_block, grad_block, slot_row, live_row, seed_row = inputs
        key_block = key_grid[slot_row].reshape(slot_count * BS, H, DH)
        value_block = value_grid[slot_row].reshape(slot_count * BS, H, DH)
        live_keys = jnp.repeat(live_row, BS)
        keep_scale = keep_weights(seed_row, BS)
        attended_block, query_block_grad, key_part, value_part = block_terms(
            query_block, key_block, value_block, grad_block, live_keys, keep_scale, score_scale)
        key_part = key_part.reshape(slot_count, BS, H, DH)
        value_part = value_part.reshape(slot_count, BS, H, DH)
        key_part = jnp.where(far_slots, rounded(key_part), key_part)
        value_part = jnp.where(far_slots, rounded(value_part), value_part)
        key_total = key_total.at[slot_row].add(key_part)
        value_total = value_total.at[slot_row].add(value_part)
        return (key_total, value_total), (attended_block, query_block_grad)

    start_totals = (jnp.zeros(grid_shape, jnp.float32), jnp.zeros(grid_shape, jnp.float32))
    totals, outputs = lax.scan(block_step, start_totals, (query_grid, grad_grid, slot_blocks, live_slots, seed_rows))
    attended = outputs[0].reshape(NODES, H * DH)
    query_grad = outputs[1].reshape(NODES, H * DH)
    key_grad = totals[0].astype(jnp.bfloat16).reshape(NODES, H * DH)
    value_grad = totals[1].astype(jnp.bfloat16).reshape(NODES, H * DH)
    return (attended, query_grad, key_grad, value_grad)
```

```python
import functools
import math

import jax
import jax.numpy as jnp
from jax import lax
from jax.experimental import pallas as pl
from jax.experimental.pallas import tpu as pltpu
from jax.sharding import PartitionSpec as P

BS = 128
QB_DEV = 8
L = 11
E = 4
W = 4
NB = 1 + L + E
DH = 64
PAIR = 2 * DH

KEEP_LEVEL = 102
KEEP_GAIN = 1024.0 / 922.0
MASKED = -1e30
LOG2E = math.log2(math.e)
CHUNK = 2 * BS
KEYS = NB * BS
FLUSH = 8


def logical_right(value, amount):
    return lax.shift_right_logical(value, jnp.full(value.shape, amount, jnp.int32))


def both_heads(rows):
    turned = rows.astype(jnp.float32).T
    upper = lax.broadcasted_iota(jnp.int32, turned.shape, 0) < DH
    return jnp.concatenate([jnp.where(upper, turned, 0.0), jnp.where(upper, 0.0, turned)], axis=1)


def one_each(wide):
    upper = lax.broadcasted_iota(jnp.int32, (PAIR, BS), 0) < DH
    return jnp.where(upper, wide[:, :BS], wide[:, BS:]).T


def dot(lhs, rhs, dims):
    return lax.dot_general(lhs, rhs, (dims, ((), ())), preferred_element_type=jnp.float32)


def attention_kernel(
    slots, live, q_ref, g_ref, kv_ref, word_ref, att_ref, dq_ref, grads_ref,
    acc, keys, values, scores, weights, kept, score_grad, stage, sems,
):
    c = pl.program_id(0)
    total_blocks = acc.shape[0]

    @pl.when(c == 0)
    def _():
        def clear(b, carry):
            acc[b] = jnp.zeros(acc.shape[1:], acc.dtype)
            return carry

        lax.fori_loop(0, total_blocks, clear, 0)

    for j in range(NB):
        keys[j * BS : (j + 1) * BS, :] = kv_ref[slots[c, j], :, :PAIR]
        values[j * BS : (j + 1) * BS, :] = kv_ref[slots[c, j], :, PAIR:]

    q_turned = (both_heads(q_ref[...]) * (DH**-0.5)).astype(jnp.bfloat16)
    g_wide = both_heads(g_ref[...])

    largest = jnp.full((8, 2 * BS), MASKED, jnp.float32)
    for at in range(0, KEYS, CHUNK):
        part = dot(keys[at : at + CHUNK, :], q_turned, ((1,), (0,)))
        if at + CHUNK > (1 + L) * BS:
            slot = at // BS + lax.broadcasted_iota(jnp.int32, part.shape, 0) // BS
            part = jnp.where(slot - (1 + L) < live[c], part, MASKED)
        scores[at : at + CHUNK, :] = part
        largest = jnp.maximum(largest, jnp.max(part.reshape(-1, 8, 2 * BS), axis=0))
    largest = jnp.max(largest, axis=0, keepdims=True)

    total = jnp.zeros((8, 2 * BS), jnp.float32)
    key_row = lax.broadcasted_iota(jnp.int32, (BS, 2 * BS), 0)
    for j in range(NB):
        rows = slice(j * BS, (j + 1) * BS)
        weight = jnp.exp2((scores[rows, :] - largest) * LOG2E)
        total = total + jnp.sum(weight.reshape(-1, 8, 2 * BS), axis=0)
        word = key_row + word_ref[0, j : j + 1, :]
        word = word ^ logical_right(word, 15)
        word = word * 739982445
        word = word ^ logical_right(word, 12)
        word = word * 695872825
        word = word ^ logical_right(word, 15)
        weights[rows, :] = weight.astype(jnp.bfloat16)
        kept[rows, :] = jnp.where((word & 1023) >= KEEP_LEVEL, weight, 0.0).astype(jnp.bfloat16)
    inverse = 1.0 / jnp.sum(total, axis=0, keepdims=True)

    out_turned = dot(values[...], kept[...], ((0,), (0,))) * (inverse * KEEP_GAIN)
    att_ref[...] = one_each(out_turned).astype(att_ref.dtype)
    delta = jnp.sum(out_turned * g_wide, axis=0, keepdims=True) * inverse
    g_turned = (g_wide * (inverse * KEEP_GAIN)).astype(jnp.bfloat16)

    for at in range(0, KEYS, CHUNK):
        rows = slice(at, at + CHUNK)
        drop_grad = dot(values[rows, :], g_turned, ((1,), (0,)))
        part = kept[rows, :]
        slope = (
            part.astype(jnp.float32) * drop_grad - weights[rows, :].astype(jnp.float32) * delta
        ).astype(jnp.bfloat16)
        score_grad[rows, :] = slope
        key_part = dot(slope, q_turned, ((1,), (1,)))
        value_part = dot(part, g_turned, ((1,), (1,)))
        for half in range(CHUNK // BS):
            here = slice(half * BS, (half + 1) * BS)
            block = slots[c, at // BS + half]
            acc[block, :, :PAIR] += key_part[here, :]
            acc[block, :, PAIR:] += value_part[here, :]
    q_grad = dot(keys[...], score_grad[...], ((0,), (0,))) * (DH**-0.5)
    dq_ref[...] = one_each(q_grad).astype(dq_ref.dtype)

    @pl.when(c == pl.num_programs(0) - 1)
    def _():
        copies = []
        for n in range(total_blocks // FLUSH):
            if n >= 2:
                copies[n - 2].wait()
            span = pl.ds(n * FLUSH, FLUSH)
            stage[n % 2] = acc[span].astype(stage.dtype)
            copy = pltpu.make_async_copy(stage.at[n % 2], grads_ref.at[span], sems.at[n % 2])
            copy.start()
            copies.append(copy)
        for copy in copies[-2:]:
            copy.wait()


def attend(slots, live, q, g, kv, words, pair):
    blocks = kv.shape[0]
    rows = q.shape[0]
    row_block = pl.BlockSpec((BS, PAIR), lambda c, s, n: (c, pair))
    out_block = pl.BlockSpec((BS, PAIR), lambda c, s, n: (c, 0))
    elements = rows * KEYS * 2
    return pl.pallas_call(
        attention_kernel,
        grid_spec=pltpu.PrefetchScalarGridSpec(
            num_scalar_prefetch=2,
            grid=(rows // BS,),
            in_specs=[
                row_block,
                row_block,
                pl.BlockSpec(
                    kv.shape, lambda c, s, n: (0, 0, 0), pipeline_mode=pl.Buffered(1)
                ),
                pl.BlockSpec((1, NB, 2 * BS), lambda c, s, n: (c, 0, 0)),
            ],
            out_specs=[out_block, out_block, pl.BlockSpec(memory_space=pl.ANY)],
            scratch_shapes=[
                pltpu.VMEM((blocks, BS, 2 * PAIR), jnp.float32),
                pltpu.VMEM((KEYS, PAIR), jnp.bfloat16),
                pltpu.VMEM((KEYS, PAIR), jnp.bfloat16),
                pltpu.VMEM((KEYS, 2 * BS), jnp.float32),
                pltpu.VMEM((KEYS, 2 * BS), jnp.bfloat16),
                pltpu.VMEM((KEYS, 2 * BS), jnp.bfloat16),
                pltpu.VMEM((KEYS, 2 * BS), jnp.bfloat16),
                pltpu.VMEM((2, FLUSH, BS, 2 * PAIR), jnp.bfloat16),
                pltpu.SemaphoreType.DMA((2,)),
            ],
        ),
        out_shape=[
            jax.ShapeDtypeStruct((rows, PAIR), jnp.bfloat16),
            jax.ShapeDtypeStruct((rows, PAIR), jnp.bfloat16),
            jax.ShapeDtypeStruct(kv.shape, jnp.bfloat16),
        ],
        compiler_params=pltpu.CompilerParams(
            dimension_semantics=("arbitrary",),
            vmem_limit_bytes=(24 << 20) + blocks * BS * 2 * PAIR * 6,
        ),
        cost_estimate=pl.CostEstimate(
            flops=elements * DH * 12 + elements * 400, bytes_accessed=16 << 20,
            transcendentals=elements,
        ),
    )(slots, live, q, g, kv, words)


def on_device(
    query_rows,
    key_rows,
    value_rows,
    out_grad,
    expander_device,
    expander_block,
    local_offset,
    live_count,
    drop_seed,
):
    head_count = lax.axis_size("head")
    share_rows = query_rows.shape[0]
    local_width = query_rows.shape[1] // head_count
    pairs = local_width // PAIR
    peer_count = lax.axis_size("blk")
    blocks = peer_count * QB_DEV
    block_rows = QB_DEV * BS

    def to_heads(members):
        sent = jnp.stack(
            [m.reshape(share_rows, head_count, local_width).transpose(1, 0, 2) for m in members],
            axis=1,
        )
        got = lax.all_to_all(sent, "head", split_axis=0, concat_axis=0, tiled=True)
        return [got[:, n].reshape(block_rows, local_width) for n in range(len(members))]

    def to_rows(members):
        sent = jnp.stack(
            [m.reshape(head_count, share_rows, m.shape[-1]) for m in members], axis=1
        )
        got = lax.all_to_all(sent, "head", split_axis=0, concat_axis=0, tiled=True)
        return [got[:, n] for n in range(len(members))]

    key_local, value_local, query_local, grad_local = to_heads(
        [key_rows, value_rows, query_rows, out_grad]
    )
    mine = lax.axis_index("blk") * QB_DEV + jnp.arange(QB_DEV, dtype=jnp.int32)[:, None]
    slots = jnp.concatenate(
        [mine, (mine + local_offset + blocks) % blocks, expander_device * QB_DEV + expander_block],
        axis=1,
    ).astype(jnp.int32)
    row = jnp.arange(BS, dtype=jnp.int32) * BS
    words = (drop_seed * 40503)[..., None] + row

    parts = []
    for pair in range(pairs):
        columns = slice(pair * PAIR, (pair + 1) * PAIR)
        kv = jnp.concatenate([key_local[:, columns], value_local[:, columns]], axis=1)
        kv = lax.all_gather(kv, "blk", axis=0, tiled=True).reshape(blocks, BS, 2 * PAIR)
        pair_words = jnp.concatenate([words[2 * pair], words[2 * pair + 1]], axis=-1)
        att, dq, grads = attend(slots, live_count, query_local, grad_local, kv, pair_words, pair)
        grads = lax.psum_scatter(
            grads.reshape(blocks * BS, 2 * PAIR), "blk", scatter_dimension=0, tiled=True
        )
        parts.append((att, dq, grads[:, :PAIR], grads[:, PAIR:]))
    locals_ = [jnp.concatenate([part[n] for part in parts], axis=1) for n in range(4)]
    out = to_rows(locals_)
    return tuple(m.transpose(1, 0, 2).reshape(share_rows, -1) for m in out)


def solution(mesh):
    rows = P(("blk", "head"), None)
    in_specs = (
        rows,
        rows,
        rows,
        rows,
        P("blk", None),
        P("blk", None),
        P("blk", None),
        P("blk"),
        P("head", "blk", None),
    )
    return jax.shard_map(
        on_device, mesh=mesh, in_specs=in_specs, out_specs=(rows,) * 4, check_vma=False
    )
```

```python
import functools
import math

import jax
import jax.numpy as jnp
from jax import lax
from jax.experimental import pallas as pl
from jax.experimental.pallas import tpu as pltpu
from jax.sharding import PartitionSpec as P

BS = 128
QB_DEV = 8
L = 11
E = 4
W = 4
NB = 1 + L + E
DH = 64
PAIR = 2 * DH

KEEP_LEVEL = 102
KEEP_GAIN = 1024.0 / 922.0
MASKED = -1e30
LOG2E = math.log2(math.e)
CHUNK = 2 * BS
KEYS = NB * BS
FLUSH = 8


def logical_right(value, amount):
    return lax.shift_right_logical(value, jnp.full(value.shape, amount, jnp.int32))


def both_heads(rows):
    turned = rows.astype(jnp.float32).T
    upper = lax.broadcasted_iota(jnp.int32, turned.shape, 0) < DH
    return jnp.concatenate([jnp.where(upper, turned, 0.0), jnp.where(upper, 0.0, turned)], axis=1)


def one_each(wide):
    upper = lax.broadcasted_iota(jnp.int32, (PAIR, BS), 0) < DH
    return jnp.where(upper, wide[:, :BS], wide[:, BS:]).T


def dot(lhs, rhs, dims):
    return lax.dot_general(lhs, rhs, (dims, ((), ())), preferred_element_type=jnp.float32)


def attention_kernel(
    slots, live, q_ref, g_ref, kv_ref, word_ref, att_ref, dq_ref, grads_ref,
    acc, keys, values, scores, weights, kept, score_grad, stage, sems,
):
    c = pl.program_id(0)
    total_blocks = acc.shape[0]

    @pl.when(c == 0)
    def _():
        def clear(b, carry):
            acc[b] = jnp.zeros(acc.shape[1:], acc.dtype)
            return carry

        lax.fori_loop(0, total_blocks, clear, 0)

    for j in range(NB):
        keys[j * BS : (j + 1) * BS, :] = kv_ref[slots[c, j], :, :PAIR]
        values[j * BS : (j + 1) * BS, :] = kv_ref[slots[c, j], :, PAIR:]

    q_turned = (both_heads(q_ref[...]) * (DH**-0.5)).astype(jnp.bfloat16)
    g_wide = both_heads(g_ref[...])

    largest = jnp.full((8, 2 * BS), MASKED, jnp.float32)
    for at in range(0, KEYS, CHUNK):
        part = dot(keys[at : at + CHUNK, :], q_turned, ((1,), (0,)))
        if at + CHUNK > (1 + L) * BS:
            slot = at // BS + lax.broadcasted_iota(jnp.int32, part.shape, 0) // BS
            part = jnp.where(slot - (1 + L) < live[c], part, MASKED)
        scores[at : at + CHUNK, :] = part
        largest = jnp.maximum(largest, jnp.max(part.reshape(-1, 8, 2 * BS), axis=0))
    largest = jnp.max(largest, axis=0, keepdims=True)

    total = jnp.zeros((8, 2 * BS), jnp.float32)
    key_row = lax.broadcasted_iota(jnp.int32, (BS, 2 * BS), 0)
    for j in range(NB):
        rows = slice(j * BS, (j + 1) * BS)
        weight = jnp.exp2((scores[rows, :] - largest) * LOG2E)
        total = total + jnp.sum(weight.reshape(-1, 8, 2 * BS), axis=0)
        word = key_row + word_ref[0, j : j + 1, :]
        word = word ^ logical_right(word, 15)
        word = word * 739982445
        word = word ^ logical_right(word, 12)
        word = word * 695872825
        word = word ^ logical_right(word, 15)
        weights[rows, :] = weight.astype(jnp.bfloat16)
        kept[rows, :] = jnp.where((word & 1023) >= KEEP_LEVEL, weight, 0.0).astype(jnp.bfloat16)
    inverse = 1.0 / jnp.sum(total, axis=0, keepdims=True)

    out_turned = dot(values[...], kept[...], ((0,), (0,))) * (inverse * KEEP_GAIN)
    att_ref[...] = one_each(out_turned).astype(att_ref.dtype)
    delta = jnp.sum(out_turned * g_wide, axis=0, keepdims=True) * inverse
    g_turned = (g_wide * (inverse * KEEP_GAIN)).astype(jnp.bfloat16)

    for at in range(0, KEYS, CHUNK):
        rows = slice(at, at + CHUNK)
        drop_grad = dot(values[rows, :], g_turned, ((1,), (0,)))
        part = kept[rows, :]
        slope = (
            part.astype(jnp.float32) * drop_grad - weights[rows, :].astype(jnp.float32) * delta
        ).astype(jnp.bfloat16)
        score_grad[rows, :] = slope
        key_part = dot(slope, q_turned, ((1,), (1,)))
        value_part = dot(part, g_turned, ((1,), (1,)))
        for half in range(CHUNK // BS):
            here = slice(half * BS, (half + 1) * BS)
            block = slots[c, at // BS + half]
            acc[block, :, :PAIR] += key_part[here, :]
            acc[block, :, PAIR:] += value_part[here, :]
    q_grad = dot(keys[...], score_grad[...], ((0,), (0,))) * (DH**-0.5)
    dq_ref[...] = one_each(q_grad).astype(dq_ref.dtype)

    @pl.when(c == pl.num_programs(0) - 1)
    def _():
        copies = []
        for n in range(total_blocks // FLUSH):
            if n >= 2:
                copies[n - 2].wait()
            span = pl.ds(n * FLUSH, FLUSH)
            stage[n % 2] = acc[span].astype(stage.dtype)
            copy = pltpu.make_async_copy(stage.at[n % 2], grads_ref.at[span], sems.at[n % 2])
            copy.start()
            copies.append(copy)
        for copy in copies[-2:]:
            copy.wait()


def attend(slots, live, q, g, kv, words, pair):
    blocks = kv.shape[0]
    rows = q.shape[0]
    row_block = pl.BlockSpec((BS, PAIR), lambda c, s, n: (c, pair))
    out_block = pl.BlockSpec((BS, PAIR), lambda c, s, n: (c, 0))
    elements = rows * KEYS * 2
    return pl.pallas_call(
        attention_kernel,
        grid_spec=pltpu.PrefetchScalarGridSpec(
            num_scalar_prefetch=2,
            grid=(rows // BS,),
            in_specs=[
                row_block,
                row_block,
                pl.BlockSpec(
                    (blocks, BS, 2 * PAIR), lambda c, s, n: (0, 0, pair), pipeline_mode=pl.Buffered(1)
                ),
                pl.BlockSpec((1, NB, 2 * BS), lambda c, s, n: (c, 0, 0)),
            ],
            out_specs=[out_block, out_block, pl.BlockSpec(memory_space=pl.ANY)],
            scratch_shapes=[
                pltpu.VMEM((blocks, BS, 2 * PAIR), jnp.float32),
                pltpu.VMEM((KEYS, PAIR), jnp.bfloat16),
                pltpu.VMEM((KEYS, PAIR), jnp.bfloat16),
                pltpu.VMEM((KEYS, 2 * BS), jnp.float32),
                pltpu.VMEM((KEYS, 2 * BS), jnp.bfloat16),
                pltpu.VMEM((KEYS, 2 * BS), jnp.bfloat16),
                pltpu.VMEM((KEYS, 2 * BS), jnp.bfloat16),
                pltpu.VMEM((2, FLUSH, BS, 2 * PAIR), jnp.bfloat16),
                pltpu.SemaphoreType.DMA((2,)),
            ],
        ),
        out_shape=[
            jax.ShapeDtypeStruct((rows, PAIR), jnp.bfloat16),
            jax.ShapeDtypeStruct((rows, PAIR), jnp.bfloat16),
            jax.ShapeDtypeStruct((blocks, BS, 2 * PAIR), jnp.bfloat16),
        ],
        compiler_params=pltpu.CompilerParams(
            dimension_semantics=("arbitrary",),
            vmem_limit_bytes=(24 << 20) + blocks * BS * 2 * PAIR * 6,
        ),
        cost_estimate=pl.CostEstimate(
            flops=elements * DH * 12 + elements * 400, bytes_accessed=16 << 20,
            transcendentals=elements,
        ),
    )(slots, live, q, g, kv, words)


MESH = pl.DeviceIdType.MESH


def ring_place(n):
    me = lax.axis_index("blk")
    half = n // 2
    z, y = me // 2, me % 2

    def index_of(place):
        place = (place + 2 * n) % n
        back = place // half
        return 2 * place * (1 - back) + (2 * (n - 1 - place) + 1) * back

    return z * (1 - y) + (n - 1 - z) * y, index_of


def meet(devices):
    barrier = pltpu.get_barrier_semaphore()
    for device in devices:
        pl.semaphore_signal(barrier, inc=1, device_id={"blk": device}, device_id_type=MESH)
    pl.semaphore_wait(barrier, len(devices))


def gather_kernel(n, mine_ref, all_ref, own_sem, send_sem, recv_sem):
    place, index_of = ring_place(n)
    beside = (index_of(place + 1), index_of(place - 1))
    meet(beside)
    own = pltpu.make_async_copy(
        mine_ref, all_ref.at[pl.ds(index_of(place) * QB_DEV, QB_DEV)], own_sem
    )
    own.start()
    size = QB_DEV // 4

    def copy_of(step, way, part):
        origin = index_of(place - step if way == 0 else place + step)
        first = (way * 2 + part) * size
        there = all_ref.at[pl.ds(origin * QB_DEV + first, size)]
        return pltpu.make_async_remote_copy(
            src_ref=mine_ref.at[pl.ds(first, size)] if step == 0 else there,
            dst_ref=there,
            send_sem=send_sem.at[way, part, step],
            recv_sem=recv_sem.at[way, part, step],
            device_id={"blk": beside[way]},
            device_id_type=MESH,
        )

    copies = {}
    for step in range(n):
        for part in range(2):
            for way in range(2):
                if step > 0:
                    copies[step - 1, way, part].wait_recv()
                if step < n - 1:
                    copies[step, way, part] = copy_of(step, way, part)
                    copies[step, way, part].start()
    for copy in copies.values():
        copy.wait_send()
    own.wait()


def gather_blocks(mine, n):
    steps = pltpu.SemaphoreType.DMA((2, 2, n - 1))
    return pl.pallas_call(
        functools.partial(gather_kernel, n),
        out_shape=jax.ShapeDtypeStruct((n * mine.shape[0],) + mine.shape[1:], mine.dtype),
        in_specs=[pl.BlockSpec(memory_space=pl.ANY)],
        out_specs=pl.BlockSpec(memory_space=pl.ANY),
        scratch_shapes=[pltpu.SemaphoreType.DMA, steps, steps],
        compiler_params=pltpu.CompilerParams(collective_id=0, has_side_effects=True),
    )(mine)


def reduce_kernel(n, pairs, *refs):
    terms, sums = refs[:pairs], refs[pairs : 2 * pairs]
    arrived, own, own_sem, send_sem, recv_sem = refs[2 * pairs :]
    place, index_of = ring_place(n)
    beside = (index_of(place + 1), index_of(place - 1))
    meet(beside)
    size = QB_DEV // 2
    lanes = [(way, pair) for pair in range(pairs) for way in range(2)]

    def term_of(step, way, pair):
        owner = index_of(place - 1 - step if way == 0 else place + 1 + step)
        return terms[pair].at[pl.ds(owner * QB_DEV + way * size, size)]

    def fetch_of(step, way, pair):
        slot = step % 2
        return pltpu.make_async_copy(
            term_of(step, way, pair), own.at[way, pair, slot], own_sem.at[way, pair, slot]
        )

    copies = {}
    fetches = {}
    for step in range(n):
        for way, pair in lanes:
            if step > 0:
                copies[step - 1, way, pair].wait_recv()
                fetches[step, way, pair].wait()
                for b in range(size):
                    got = arrived[way, pair, step - 1, b].astype(jnp.float32)
                    got = (got + own[way, pair, step % 2, b].astype(jnp.float32)).astype(
                        jnp.bfloat16
                    )
                    if step < n - 1:
                        arrived[way, pair, step - 1, b] = got
                    else:
                        sums[pair][way * size + b] = got
            if step < n - 1:
                copies[step, way, pair] = pltpu.make_async_remote_copy(
                    src_ref=term_of(0, way, pair) if step == 0 else arrived.at[way, pair, step - 1],
                    dst_ref=arrived.at[way, pair, step],
                    send_sem=send_sem.at[way, pair, step],
                    recv_sem=recv_sem.at[way, pair, step],
                    device_id={"blk": beside[way]},
                    device_id_type=MESH,
                )
                copies[step, way, pair].start()
                fetches[step + 1, way, pair] = fetch_of(step + 1, way, pair)
                fetches[step + 1, way, pair].start()
    for copy in copies.values():
        copy.wait_send()


def reduce_blocks(terms, n):
    pairs = len(terms)
    tail = terms[0].shape[1:]
    chunk = (QB_DEV // 2,) + tail
    steps = pltpu.SemaphoreType.DMA((2, pairs, n - 1))
    return pl.pallas_call(
        functools.partial(reduce_kernel, n, pairs),
        out_shape=[jax.ShapeDtypeStruct((QB_DEV,) + tail, jnp.bfloat16)] * pairs,
        in_specs=[pl.BlockSpec(memory_space=pl.ANY)] * pairs,
        out_specs=[pl.BlockSpec(memory_space=pltpu.VMEM)] * pairs,
        scratch_shapes=[
            pltpu.VMEM((2, pairs, n - 1) + chunk, jnp.bfloat16),
            pltpu.VMEM((2, pairs, 2) + chunk, jnp.bfloat16),
            pltpu.SemaphoreType.DMA((2, pairs, 2)),
            steps,
            steps,
        ],
        compiler_params=pltpu.CompilerParams(
            collective_id=1, has_side_effects=True, vmem_limit_bytes=(n + 12) << 20
        ),
    )(*terms)


def on_device(
    query_rows,
    key_rows,
    value_rows,
    out_grad,
    expander_device,
    expander_block,
    local_offset,
    live_count,
    drop_seed,
):
    head_count = lax.axis_size("head")
    share_rows = query_rows.shape[0]
    local_width = query_rows.shape[1] // head_count
    pairs = local_width // PAIR
    peer_count = lax.axis_size("blk")
    blocks = peer_count * QB_DEV
    block_rows = QB_DEV * BS

    def to_heads(members):
        sent = jnp.stack(
            [m.reshape(share_rows, head_count, local_width).transpose(1, 0, 2) for m in members],
            axis=1,
        )
        got = lax.all_to_all(sent, "head", split_axis=0, concat_axis=0, tiled=True)
        return [got[:, n].reshape(block_rows, local_width) for n in range(len(members))]

    def to_rows(members):
        sent = jnp.stack(
            [m.reshape(head_count, share_rows, m.shape[-1]) for m in members], axis=1
        )
        got = lax.all_to_all(sent, "head", split_axis=0, concat_axis=0, tiled=True)
        return [got[:, n] for n in range(len(members))]

    key_local, value_local, query_local, grad_local = to_heads(
        [key_rows, value_rows, query_rows, out_grad]
    )
    mine = lax.axis_index("blk") * QB_DEV + jnp.arange(QB_DEV, dtype=jnp.int32)[:, None]
    slots = jnp.concatenate(
        [mine, (mine + local_offset + blocks) % blocks, expander_device * QB_DEV + expander_block],
        axis=1,
    ).astype(jnp.int32)
    row = jnp.arange(BS, dtype=jnp.int32) * BS
    words = (drop_seed * 40503)[..., None] + row

    mixed = []
    for pair in range(pairs):
        columns = slice(pair * PAIR, (pair + 1) * PAIR)
        mixed += [key_local[:, columns], value_local[:, columns]]
    mixed = jnp.concatenate(mixed, axis=1).reshape(QB_DEV, BS, pairs * 2 * PAIR)
    kv = gather_blocks(mixed, peer_count)
    parts, terms = [], []
    for pair in range(pairs):
        pair_words = jnp.concatenate([words[2 * pair], words[2 * pair + 1]], axis=-1)
        att, dq, grads = attend(slots, live_count, query_local, grad_local, kv, pair_words, pair)
        parts.append((att, dq))
        terms.append(grads)
    sums = [m.reshape(block_rows, 2 * PAIR) for m in reduce_blocks(terms, peer_count)]
    locals_ = [jnp.concatenate([part[n] for part in parts], axis=1) for n in range(2)]
    locals_.append(jnp.concatenate([m[:, :PAIR] for m in sums], axis=1))
    locals_.append(jnp.concatenate([m[:, PAIR:] for m in sums], axis=1))
    out = to_rows(locals_)
    return tuple(m.transpose(1, 0, 2).reshape(share_rows, -1) for m in out)


def solution(mesh):
    rows = P(("blk", "head"), None)
    in_specs = (
        rows,
        rows,
        rows,
        rows,
        P("blk", None),
        P("blk", None),
        P("blk", None),
        P("blk"),
        P("head", "blk", None),
    )
    return jax.shard_map(
        on_device, mesh=mesh, in_specs=in_specs, out_specs=(rows,) * 4, check_vma=False
    )
```

```python
import functools
import math

import jax
import jax.numpy as jnp
from jax import lax
from jax.experimental import pallas as pl
from jax.experimental.pallas import tpu as pltpu
from jax.sharding import PartitionSpec as P

BS = 128
QB_DEV = 8
L = 11
E = 4
W = 4
NB = 1 + L + E
DH = 64
PAIR = 2 * DH

KEEP_LEVEL = 102
KEEP_GAIN = 1024.0 / 922.0
MASKED = -1e30
LOG2E = math.log2(math.e)
CHUNK = 2 * BS
KEYS = NB * BS
FLUSH = 8


def logical_right(value, amount):
    return lax.shift_right_logical(value, jnp.full(value.shape, amount, jnp.int32))


def both_heads(rows):
    turned = rows.astype(jnp.float32).T
    upper = lax.broadcasted_iota(jnp.int32, turned.shape, 0) < DH
    return jnp.concatenate([jnp.where(upper, turned, 0.0), jnp.where(upper, 0.0, turned)], axis=1)


def one_each(wide):
    upper = lax.broadcasted_iota(jnp.int32, (PAIR, BS), 0) < DH
    return jnp.where(upper, wide[:, :BS], wide[:, BS:]).T


def dot(lhs, rhs, dims):
    return lax.dot_general(lhs, rhs, (dims, ((), ())), preferred_element_type=jnp.float32)


def attention_kernel(
    slots, live, q_ref, g_ref, kv_ref, word_ref, att_ref, dq_ref, grads_ref,
    acc, keys, values, scores, weights, kept, score_grad, stage, sems,
):
    c = pl.program_id(0)
    total_blocks = acc.shape[0]

    @pl.when(c == 0)
    def _():
        def clear(b, carry):
            acc[b] = jnp.zeros(acc.shape[1:], acc.dtype)
            return carry

        lax.fori_loop(0, total_blocks, clear, 0)

    for j in range(NB):
        keys[j * BS : (j + 1) * BS, :] = kv_ref[slots[c, j], :, :PAIR]
        values[j * BS : (j + 1) * BS, :] = kv_ref[slots[c, j], :, PAIR:]

    q_turned = (both_heads(q_ref[...]) * (DH**-0.5)).astype(jnp.bfloat16)
    g_wide = both_heads(g_ref[...])

    largest = jnp.full((8, 2 * BS), MASKED, jnp.float32)
    for at in range(0, KEYS, CHUNK):
        part = dot(keys[at : at + CHUNK, :], q_turned, ((1,), (0,)))
        if at + CHUNK > (1 + L) * BS:
            slot = at // BS + lax.broadcasted_iota(jnp.int32, part.shape, 0) // BS
            part = jnp.where(slot - (1 + L) < live[c], part, MASKED)
        scores[at : at + CHUNK, :] = part
        largest = jnp.maximum(largest, jnp.max(part.reshape(-1, 8, 2 * BS), axis=0))
    largest = jnp.max(largest, axis=0, keepdims=True)

    total = jnp.zeros((8, 2 * BS), jnp.float32)
    key_row = lax.broadcasted_iota(jnp.int32, (BS, 2 * BS), 0)
    for j in range(NB):
        rows = slice(j * BS, (j + 1) * BS)
        weight = jnp.exp2((scores[rows, :] - largest) * LOG2E)
        total = total + jnp.sum(weight.reshape(-1, 8, 2 * BS), axis=0)
        word = key_row + word_ref[0, j : j + 1, :]
        word = word ^ logical_right(word, 15)
        word = word * 739982445
        word = word ^ logical_right(word, 12)
        word = word * 695872825
        word = word ^ logical_right(word, 15)
        weights[rows, :] = weight.astype(jnp.bfloat16)
        kept[rows, :] = jnp.where((word & 1023) >= KEEP_LEVEL, weight, 0.0).astype(jnp.bfloat16)
    inverse = 1.0 / jnp.sum(total, axis=0, keepdims=True)

    out_turned = dot(values[...], kept[...], ((0,), (0,))) * (inverse * KEEP_GAIN)
    att_ref[...] = one_each(out_turned).astype(att_ref.dtype)
    delta = jnp.sum(out_turned * g_wide, axis=0, keepdims=True) * inverse
    g_turned = (g_wide * (inverse * KEEP_GAIN)).astype(jnp.bfloat16)

    for at in range(0, KEYS, CHUNK):
        rows = slice(at, at + CHUNK)
        drop_grad = dot(values[rows, :], g_turned, ((1,), (0,)))
        part = kept[rows, :]
        slope = (
            part.astype(jnp.float32) * drop_grad - weights[rows, :].astype(jnp.float32) * delta
        ).astype(jnp.bfloat16)
        score_grad[rows, :] = slope
        key_part = dot(slope, q_turned, ((1,), (1,)))
        value_part = dot(part, g_turned, ((1,), (1,)))
        for half in range(CHUNK // BS):
            here = slice(half * BS, (half + 1) * BS)
            block = slots[c, at // BS + half]
            acc[block, :, :PAIR] += key_part[here, :]
            acc[block, :, PAIR:] += value_part[here, :]
    q_grad = dot(keys[...], score_grad[...], ((0,), (0,))) * (DH**-0.5)
    dq_ref[...] = one_each(q_grad).astype(dq_ref.dtype)

    @pl.when(c == pl.num_programs(0) - 1)
    def _():
        copies = []
        for n in range(total_blocks // FLUSH):
            if n >= 2:
                copies[n - 2].wait()
            span = pl.ds(n * FLUSH, FLUSH)
            stage[n % 2] = acc[span].astype(stage.dtype)
            copy = pltpu.make_async_copy(stage.at[n % 2], grads_ref.at[span], sems.at[n % 2])
            copy.start()
            copies.append(copy)
        for copy in copies[-2:]:
            copy.wait()


def attend(slots, live, q, g, kv, words, pair):
    blocks = kv.shape[0]
    rows = q.shape[0]
    row_block = pl.BlockSpec((BS, PAIR), lambda c, s, n: (c, pair))
    out_block = pl.BlockSpec((BS, PAIR), lambda c, s, n: (c, 0))
    elements = rows * KEYS * 2
    return pl.pallas_call(
        attention_kernel,
        grid_spec=pltpu.PrefetchScalarGridSpec(
            num_scalar_prefetch=2,
            grid=(rows // BS,),
            in_specs=[
                row_block,
                row_block,
                pl.BlockSpec(
                    (blocks, BS, 2 * PAIR), lambda c, s, n: (0, 0, pair), pipeline_mode=pl.Buffered(1)
                ),
                pl.BlockSpec((1, NB, 2 * BS), lambda c, s, n: (c, 0, 0)),
            ],
            out_specs=[out_block, out_block, pl.BlockSpec(memory_space=pl.ANY)],
            scratch_shapes=[
                pltpu.VMEM((blocks, BS, 2 * PAIR), jnp.float32),
                pltpu.VMEM((KEYS, PAIR), jnp.bfloat16),
                pltpu.VMEM((KEYS, PAIR), jnp.bfloat16),
                pltpu.VMEM((KEYS, 2 * BS), jnp.float32),
                pltpu.VMEM((KEYS, 2 * BS), jnp.bfloat16),
                pltpu.VMEM((KEYS, 2 * BS), jnp.bfloat16),
                pltpu.VMEM((KEYS, 2 * BS), jnp.bfloat16),
                pltpu.VMEM((2, FLUSH, BS, 2 * PAIR), jnp.bfloat16),
                pltpu.SemaphoreType.DMA((2,)),
            ],
        ),
        out_shape=[
            jax.ShapeDtypeStruct((rows, PAIR), jnp.bfloat16),
            jax.ShapeDtypeStruct((rows, PAIR), jnp.bfloat16),
            jax.ShapeDtypeStruct((blocks, BS, 2 * PAIR), jnp.bfloat16),
        ],
        compiler_params=pltpu.CompilerParams(
            dimension_semantics=("arbitrary",),
            vmem_limit_bytes=(24 << 20) + blocks * BS * 2 * PAIR * 6,
        ),
        cost_estimate=pl.CostEstimate(
            flops=elements * DH * 12 + elements * 400, bytes_accessed=16 << 20,
            transcendentals=elements,
        ),
    )(slots, live, q, g, kv, words)


MESH = pl.DeviceIdType.MESH


def ring_place(n):
    me = lax.axis_index("blk")
    half = n // 2
    z, y = me // 2, me % 2

    def index_of(place):
        place = (place + 2 * n) % n
        back = place // half
        return 2 * place * (1 - back) + (2 * (n - 1 - place) + 1) * back

    return z * (1 - y) + (n - 1 - z) * y, index_of


def meet(beside, heads):
    barrier = pltpu.get_barrier_semaphore()
    devices = [{"blk": device} for device in beside]
    devices += [{"head": (lax.axis_index("head") + k) % heads} for k in range(1, heads)]
    for device in devices:
        pl.semaphore_signal(barrier, inc=1, device_id=device, device_id_type=MESH)
    pl.semaphore_wait(barrier, len(devices))


def exchange(heads, sent_ref, got_ref, own_sem, send_sem, recv_sem):
    me = lax.axis_index("head")
    started = [pltpu.make_async_copy(sent_ref.at[me], got_ref.at[me], own_sem)]
    for k in range(1, heads):
        peer = (me + k) % heads
        started.append(
            pltpu.make_async_remote_copy(
                src_ref=sent_ref.at[peer],
                dst_ref=got_ref.at[me],
                send_sem=send_sem.at[k - 1],
                recv_sem=recv_sem.at[k - 1],
                device_id={"head": peer},
                device_id_type=MESH,
            )
        )
    for copy in started:
        copy.start()
    return started


def exchange_semaphores(heads):
    steps = pltpu.SemaphoreType.DMA((heads - 1,))
    return [pltpu.SemaphoreType.DMA, steps, steps]


def gather_kernel(
    n, heads, mine_ref, sent_ref, all_ref, got_ref, own_sem, send_sem, recv_sem, *head_sems
):
    place, index_of = ring_place(n)
    beside = (index_of(place + 1), index_of(place - 1))
    meet(beside, heads)
    own = pltpu.make_async_copy(
        mine_ref, all_ref.at[pl.ds(index_of(place) * QB_DEV, QB_DEV)], own_sem
    )
    own.start()
    size = QB_DEV // 4

    def copy_of(step, way, part):
        origin = index_of(place - step if way == 0 else place + step)
        first = (way * 2 + part) * size
        there = all_ref.at[pl.ds(origin * QB_DEV + first, size)]
        return pltpu.make_async_remote_copy(
            src_ref=mine_ref.at[pl.ds(first, size)] if step == 0 else there,
            dst_ref=there,
            send_sem=send_sem.at[way, part, step],
            recv_sem=recv_sem.at[way, part, step],
            device_id={"blk": beside[way]},
            device_id_type=MESH,
        )

    swaps = []
    copies = {}
    for step in range(n):
        if step == 1:
            swaps = exchange(heads, sent_ref, got_ref, *head_sems)
        for part in range(2):
            for way in range(2):
                if step > 0:
                    copies[step - 1, way, part].wait_recv()
                if step < n - 1:
                    copies[step, way, part] = copy_of(step, way, part)
                    copies[step, way, part].start()
    for copy in copies.values():
        copy.wait_send()
    own.wait()
    for copy in swaps:
        copy.wait()


def gather_blocks(mine, sent, n):
    steps = pltpu.SemaphoreType.DMA((2, 2, n - 1))
    return pl.pallas_call(
        functools.partial(gather_kernel, n, sent.shape[0]),
        out_shape=[
            jax.ShapeDtypeStruct((n * mine.shape[0],) + mine.shape[1:], mine.dtype),
            jax.ShapeDtypeStruct(sent.shape, sent.dtype),
        ],
        in_specs=[pl.BlockSpec(memory_space=pl.ANY)] * 2,
        out_specs=[pl.BlockSpec(memory_space=pl.ANY)] * 2,
        scratch_shapes=[pltpu.SemaphoreType.DMA, steps, steps]
        + exchange_semaphores(sent.shape[0]),
        compiler_params=pltpu.CompilerParams(collective_id=0, has_side_effects=True),
    )(mine, sent)


def reduce_kernel(n, pairs, heads, sent_ref, *refs):
    terms, got_ref, sums = refs[:pairs], refs[pairs], refs[pairs + 1 : 2 * pairs + 1]
    arrived, own, own_sem, send_sem, recv_sem, *head_sems = refs[2 * pairs + 1 :]
    place, index_of = ring_place(n)
    beside = (index_of(place + 1), index_of(place - 1))
    meet(beside, heads)
    size = QB_DEV // 2
    lanes = [(way, pair) for pair in range(pairs) for way in range(2)]

    def term_of(step, way, pair):
        owner = index_of(place - 1 - step if way == 0 else place + 1 + step)
        return terms[pair].at[pl.ds(owner * QB_DEV + way * size, size)]

    def fetch_of(step, way, pair):
        slot = step % 2
        return pltpu.make_async_copy(
            term_of(step, way, pair), own.at[way, pair, slot], own_sem.at[way, pair, slot]
        )

    swaps = []
    copies = {}
    fetches = {}
    for step in range(n):
        if step == 1:
            swaps = exchange(heads, sent_ref, got_ref, *head_sems)
        for way, pair in lanes:
            if step > 0:
                copies[step - 1, way, pair].wait_recv()
                fetches[step, way, pair].wait()
                for b in range(size):
                    got = arrived[way, pair, step - 1, b].astype(jnp.float32)
                    got = (got + own[way, pair, step % 2, b].astype(jnp.float32)).astype(
                        jnp.bfloat16
                    )
                    if step < n - 1:
                        arrived[way, pair, step - 1, b] = got
                    else:
                        sums[pair][way * size + b] = got
            if step < n - 1:
                copies[step, way, pair] = pltpu.make_async_remote_copy(
                    src_ref=term_of(0, way, pair) if step == 0 else arrived.at[way, pair, step - 1],
                    dst_ref=arrived.at[way, pair, step],
                    send_sem=send_sem.at[way, pair, step],
                    recv_sem=recv_sem.at[way, pair, step],
                    device_id={"blk": beside[way]},
                    device_id_type=MESH,
                )
                copies[step, way, pair].start()
                fetches[step + 1, way, pair] = fetch_of(step + 1, way, pair)
                fetches[step + 1, way, pair].start()
    for copy in copies.values():
        copy.wait_send()
    for copy in swaps:
        copy.wait()


def reduce_blocks(sent, terms, n):
    pairs = len(terms)
    tail = terms[0].shape[1:]
    chunk = (QB_DEV // 2,) + tail
    steps = pltpu.SemaphoreType.DMA((2, pairs, n - 1))
    return pl.pallas_call(
        functools.partial(reduce_kernel, n, pairs, sent.shape[0]),
        out_shape=[jax.ShapeDtypeStruct(sent.shape, sent.dtype)]
        + [jax.ShapeDtypeStruct((QB_DEV,) + tail, jnp.bfloat16)] * pairs,
        in_specs=[pl.BlockSpec(memory_space=pl.ANY)] * (pairs + 1),
        out_specs=[pl.BlockSpec(memory_space=pl.ANY)]
        + [pl.BlockSpec(memory_space=pltpu.VMEM)] * pairs,
        scratch_shapes=[
            pltpu.VMEM((2, pairs, n - 1) + chunk, jnp.bfloat16),
            pltpu.VMEM((2, pairs, 2) + chunk, jnp.bfloat16),
            pltpu.SemaphoreType.DMA((2, pairs, 2)),
            steps,
            steps,
        ]
        + exchange_semaphores(sent.shape[0]),
        compiler_params=pltpu.CompilerParams(
            collective_id=1, has_side_effects=True, vmem_limit_bytes=(n + 12) << 20
        ),
    )(sent, *terms)


def on_device(
    query_rows,
    key_rows,
    value_rows,
    out_grad,
    expander_device,
    expander_block,
    local_offset,
    live_count,
    drop_seed,
):
    head_count = lax.axis_size("head")
    share_rows = query_rows.shape[0]
    local_width = query_rows.shape[1] // head_count
    pairs = local_width // PAIR
    peer_count = lax.axis_size("blk")
    blocks = peer_count * QB_DEV
    block_rows = QB_DEV * BS

    def for_heads(members):
        return jnp.stack(
            [m.reshape(share_rows, head_count, local_width).transpose(1, 0, 2) for m in members],
            axis=1,
        )

    def for_rows(members):
        return jnp.stack([m.reshape(head_count, share_rows, m.shape[-1]) for m in members], axis=1)

    def swapped(sent):
        return lax.all_to_all(sent, "head", split_axis=0, concat_axis=0, tiled=True)

    def as_blocks(got):
        return [got[:, n].reshape(block_rows, local_width) for n in range(got.shape[1])]

    def as_rows(got):
        return [got[:, n].transpose(1, 0, 2).reshape(share_rows, -1) for n in range(got.shape[1])]

    key_local, value_local = as_blocks(swapped(for_heads([key_rows, value_rows])))
    mine = lax.axis_index("blk") * QB_DEV + jnp.arange(QB_DEV, dtype=jnp.int32)[:, None]
    slots = jnp.concatenate(
        [mine, (mine + local_offset + blocks) % blocks, expander_device * QB_DEV + expander_block],
        axis=1,
    ).astype(jnp.int32)
    row = jnp.arange(BS, dtype=jnp.int32) * BS
    words = (drop_seed * 40503)[..., None] + row

    mixed = []
    for pair in range(pairs):
        columns = slice(pair * PAIR, (pair + 1) * PAIR)
        mixed += [key_local[:, columns], value_local[:, columns]]
    mixed = jnp.concatenate(mixed, axis=1).reshape(QB_DEV, BS, pairs * 2 * PAIR)
    kv, got = gather_blocks(mixed, for_heads([query_rows, out_grad]), peer_count)
    query_local, grad_local = as_blocks(got)
    parts, terms = [], []
    for pair in range(pairs):
        pair_words = jnp.concatenate([words[2 * pair], words[2 * pair + 1]], axis=-1)
        att, dq, grads = attend(slots, live_count, query_local, grad_local, kv, pair_words, pair)
        parts.append((att, dq))
        terms.append(grads)
    row_results = [jnp.concatenate([part[n] for part in parts], axis=1) for n in range(2)]
    got, *sums = reduce_blocks(for_rows(row_results), terms, peer_count)
    sums = [m.reshape(block_rows, 2 * PAIR) for m in sums]
    grads = [
        jnp.concatenate([m[:, :PAIR] for m in sums], axis=1),
        jnp.concatenate([m[:, PAIR:] for m in sums], axis=1),
    ]
    return tuple(as_rows(got) + as_rows(swapped(for_rows(grads))))


def solution(mesh):
    rows = P(("blk", "head"), None)
    in_specs = (
        rows,
        rows,
        rows,
        rows,
        P("blk", None),
        P("blk", None),
        P("blk", None),
        P("blk"),
        P("head", "blk", None),
    )
    return jax.shard_map(
        on_device, mesh=mesh, in_specs=in_specs, out_specs=(rows,) * 4, check_vma=False
    )
```

```python
import functools
import math

import jax
import jax.numpy as jnp
from jax import lax
from jax.experimental import pallas as pl
from jax.experimental.pallas import tpu as pltpu
from jax.sharding import PartitionSpec as P

BS = 128
QB_DEV = 8
L = 11
E = 4
W = 4
NB = 1 + L + E
DH = 64
PAIR = 2 * DH

KEEP_LEVEL = 102
KEEP_GAIN = 1024.0 / 922.0
MASKED = -1e30
LOG2E = math.log2(math.e)
CHUNK = 2 * BS
KEYS = NB * BS
FLUSH = 8


def logical_right(value, amount):
    return lax.shift_right_logical(value, jnp.full(value.shape, amount, jnp.int32))


def both_heads(rows):
    turned = rows.astype(jnp.float32).T
    upper = lax.broadcasted_iota(jnp.int32, turned.shape, 0) < DH
    return jnp.concatenate([jnp.where(upper, turned, 0.0), jnp.where(upper, 0.0, turned)], axis=1)


def one_each(wide):
    upper = lax.broadcasted_iota(jnp.int32, (PAIR, BS), 0) < DH
    return jnp.where(upper, wide[:, :BS], wide[:, BS:]).T


def dot(lhs, rhs, dims):
    return lax.dot_general(lhs, rhs, (dims, ((), ())), preferred_element_type=jnp.float32)


def attention_kernel(
    slots, live, q_ref, g_ref, kv_ref, word_ref, att_ref, dq_ref, grads_ref,
    acc, keys, values, scores, weights, kept, score_grad, stage, sems,
):
    c = pl.program_id(0)
    total_blocks = acc.shape[0]

    @pl.when(c == 0)
    def _():
        def clear(b, carry):
            acc[b] = jnp.zeros(acc.shape[1:], acc.dtype)
            return carry

        lax.fori_loop(0, total_blocks, clear, 0)

    for j in range(NB):
        keys[j * BS : (j + 1) * BS, :] = kv_ref[slots[c, j], :, :PAIR]
        values[j * BS : (j + 1) * BS, :] = kv_ref[slots[c, j], :, PAIR:]

    q_turned = (both_heads(q_ref[...]) * (DH**-0.5)).astype(jnp.bfloat16)
    g_wide = both_heads(g_ref[...])

    largest = jnp.full((8, 2 * BS), MASKED, jnp.float32)
    for at in range(0, KEYS, CHUNK):
        part = dot(keys[at : at + CHUNK, :], q_turned, ((1,), (0,)))
        if at + CHUNK > (1 + L) * BS:
            slot = at // BS + lax.broadcasted_iota(jnp.int32, part.shape, 0) // BS
            part = jnp.where(slot - (1 + L) < live[c], part, MASKED)
        scores[at : at + CHUNK, :] = part
        largest = jnp.maximum(largest, jnp.max(part.reshape(-1, 8, 2 * BS), axis=0))
    largest = jnp.max(largest, axis=0, keepdims=True)

    total = jnp.zeros((8, 2 * BS), jnp.float32)
    key_row = lax.broadcasted_iota(jnp.int32, (BS, 2 * BS), 0)
    for j in range(NB):
        rows = slice(j * BS, (j + 1) * BS)
        weight = jnp.exp2((scores[rows, :] - largest) * LOG2E)
        total = total + jnp.sum(weight.reshape(-1, 8, 2 * BS), axis=0)
        word = key_row + word_ref[0, j : j + 1, :]
        word = word ^ logical_right(word, 15)
        word = word * 739982445
        word = word ^ logical_right(word, 12)
        word = word * 695872825
        word = word ^ logical_right(word, 15)
        weights[rows, :] = weight.astype(jnp.bfloat16)
        kept[rows, :] = jnp.where((word & 1023) >= KEEP_LEVEL, weight, 0.0).astype(jnp.bfloat16)
    inverse = 1.0 / jnp.sum(total, axis=0, keepdims=True)

    out_turned = dot(values[...], kept[...], ((0,), (0,))) * (inverse * KEEP_GAIN)
    att_ref[...] = one_each(out_turned).astype(att_ref.dtype)
    delta = jnp.sum(out_turned * g_wide, axis=0, keepdims=True) * inverse
    g_turned = (g_wide * (inverse * KEEP_GAIN)).astype(jnp.bfloat16)

    for at in range(0, KEYS, CHUNK):
        rows = slice(at, at + CHUNK)
        drop_grad = dot(values[rows, :], g_turned, ((1,), (0,)))
        part = kept[rows, :]
        slope = (
            part.astype(jnp.float32) * drop_grad - weights[rows, :].astype(jnp.float32) * delta
        ).astype(jnp.bfloat16)
        score_grad[rows, :] = slope
        key_part = dot(slope, q_turned, ((1,), (1,)))
        value_part = dot(part, g_turned, ((1,), (1,)))
        for half in range(CHUNK // BS):
            here = slice(half * BS, (half + 1) * BS)
            block = slots[c, at // BS + half]
            acc[block, :, :PAIR] += key_part[here, :]
            acc[block, :, PAIR:] += value_part[here, :]
    q_grad = dot(keys[...], score_grad[...], ((0,), (0,))) * (DH**-0.5)
    dq_ref[...] = one_each(q_grad).astype(dq_ref.dtype)

    @pl.when(c == pl.num_programs(0) - 1)
    def _():
        copies = []
        for n in range(total_blocks // FLUSH):
            if n >= 2:
                copies[n - 2].wait()
            span = pl.ds(n * FLUSH, FLUSH)
            stage[n % 2] = acc[span].astype(stage.dtype)
            copy = pltpu.make_async_copy(stage.at[n % 2], grads_ref.at[span], sems.at[n % 2])
            copy.start()
            copies.append(copy)
        for copy in copies[-2:]:
            copy.wait()


def attend(slots, live, q, g, kv, words, pair):
    blocks = kv.shape[0]
    rows = q.shape[0]
    row_block = pl.BlockSpec((BS, PAIR), lambda c, s, n: (c, pair))
    out_block = pl.BlockSpec((BS, PAIR), lambda c, s, n: (c, 0))
    elements = rows * KEYS * 2
    return pl.pallas_call(
        attention_kernel,
        grid_spec=pltpu.PrefetchScalarGridSpec(
            num_scalar_prefetch=2,
            grid=(rows // BS,),
            in_specs=[
                row_block,
                row_block,
                pl.BlockSpec(
                    (blocks, BS, 2 * PAIR), lambda c, s, n: (0, 0, pair), pipeline_mode=pl.Buffered(1)
                ),
                pl.BlockSpec((1, NB, 2 * BS), lambda c, s, n: (c, 0, 0)),
            ],
            out_specs=[out_block, out_block, pl.BlockSpec(memory_space=pl.ANY)],
            scratch_shapes=[
                pltpu.VMEM((blocks, BS, 2 * PAIR), jnp.float32),
                pltpu.VMEM((KEYS, PAIR), jnp.bfloat16),
                pltpu.VMEM((KEYS, PAIR), jnp.bfloat16),
                pltpu.VMEM((KEYS, 2 * BS), jnp.float32),
                pltpu.VMEM((KEYS, 2 * BS), jnp.bfloat16),
                pltpu.VMEM((KEYS, 2 * BS), jnp.bfloat16),
                pltpu.VMEM((KEYS, 2 * BS), jnp.bfloat16),
                pltpu.VMEM((2, FLUSH, BS, 2 * PAIR), jnp.bfloat16),
                pltpu.SemaphoreType.DMA((2,)),
            ],
        ),
        out_shape=[
            jax.ShapeDtypeStruct((rows, PAIR), jnp.bfloat16),
            jax.ShapeDtypeStruct((rows, PAIR), jnp.bfloat16),
            jax.ShapeDtypeStruct((blocks, BS, 2 * PAIR), jnp.bfloat16),
        ],
        compiler_params=pltpu.CompilerParams(
            dimension_semantics=("arbitrary",),
            vmem_limit_bytes=(24 << 20) + blocks * BS * 2 * PAIR * 6,
        ),
        cost_estimate=pl.CostEstimate(
            flops=elements * DH * 12 + elements * 400, bytes_accessed=16 << 20,
            transcendentals=elements,
        ),
    )(slots, live, q, g, kv, words)


MESH = pl.DeviceIdType.MESH


def ring_place(n):
    me = lax.axis_index("blk")
    half = n // 2
    z, y = me // 2, me % 2

    def index_of(place):
        place = (place + 2 * n) % n
        back = place // half
        return 2 * place * (1 - back) + (2 * (n - 1 - place) + 1) * back

    return z * (1 - y) + (n - 1 - z) * y, index_of


def meet(beside, heads):
    barrier = pltpu.get_barrier_semaphore()
    devices = [{"blk": device} for device in beside]
    devices += [{"head": (lax.axis_index("head") + k) % heads} for k in range(1, heads)]
    for device in devices:
        pl.semaphore_signal(barrier, inc=1, device_id=device, device_id_type=MESH)
    pl.semaphore_wait(barrier, len(devices))


def exchange(heads, sent_ref, landing, own_sem, send_sem, recv_sem):
    me = lax.axis_index("head")
    started = [pltpu.make_async_copy(sent_ref.at[me], landing, own_sem)]
    for k in range(1, heads):
        peer = (me + k) % heads
        started.append(
            pltpu.make_async_remote_copy(
                src_ref=sent_ref.at[peer],
                dst_ref=landing,
                send_sem=send_sem.at[k - 1],
                recv_sem=recv_sem.at[k - 1],
                device_id={"head": peer},
                device_id_type=MESH,
            )
        )
    for copy in started:
        copy.start()
    return started


def exchange_semaphores(heads):
    steps = pltpu.SemaphoreType.DMA((heads - 1,))
    return [pltpu.SemaphoreType.DMA, steps, steps]


def gather_kernel(
    n, heads, mine_ref, sent_ref, all_ref, got_ref, send_sem, recv_sem, *sems
):
    place, index_of = ring_place(n)
    beside = (index_of(place + 1), index_of(place - 1))
    meet(beside, heads)
    first_sems, head_sems = sems[:3], sems[3:]
    share = QB_DEV // heads
    landing = all_ref.at[
        pl.ds(lax.axis_index("blk") * QB_DEV + lax.axis_index("head") * share, share)
    ]
    for copy in exchange(heads, mine_ref, landing, *first_sems):
        copy.wait()
    size = QB_DEV // 4

    def copy_of(step, way, part):
        origin = index_of(place - step if way == 0 else place + step)
        first = (way * 2 + part) * size
        there = all_ref.at[pl.ds(origin * QB_DEV + first, size)]
        return pltpu.make_async_remote_copy(
            src_ref=there,
            dst_ref=there,
            send_sem=send_sem.at[way, part, step],
            recv_sem=recv_sem.at[way, part, step],
            device_id={"blk": beside[way]},
            device_id_type=MESH,
        )

    swaps = []
    copies = {}
    for step in range(n):
        if step == 1:
            swaps = exchange(heads, sent_ref, got_ref.at[lax.axis_index("head")], *head_sems)
        for part in range(2):
            for way in range(2):
                if step > 0:
                    copies[step - 1, way, part].wait_recv()
                if step < n - 1:
                    copies[step, way, part] = copy_of(step, way, part)
                    copies[step, way, part].start()
    for copy in copies.values():
        copy.wait_send()
    for copy in swaps:
        copy.wait()


def gather_blocks(mine, sent, n):
    steps = pltpu.SemaphoreType.DMA((2, 2, n - 1))
    return pl.pallas_call(
        functools.partial(gather_kernel, n, sent.shape[0]),
        out_shape=[
            jax.ShapeDtypeStruct((n * QB_DEV,) + mine.shape[2:], mine.dtype),
            jax.ShapeDtypeStruct(sent.shape, sent.dtype),
        ],
        in_specs=[pl.BlockSpec(memory_space=pl.ANY)] * 2,
        out_specs=[pl.BlockSpec(memory_space=pl.ANY)] * 2,
        scratch_shapes=[steps, steps]
        + exchange_semaphores(sent.shape[0])
        + exchange_semaphores(sent.shape[0]),
        compiler_params=pltpu.CompilerParams(collective_id=0, has_side_effects=True),
    )(mine, sent)


def reduce_kernel(n, pairs, heads, sent_ref, *refs):
    terms, got_ref, sums = refs[:pairs], refs[pairs], refs[pairs + 1 : 2 * pairs + 1]
    arrived, own, own_sem, send_sem, recv_sem, *head_sems = refs[2 * pairs + 1 :]
    place, index_of = ring_place(n)
    beside = (index_of(place + 1), index_of(place - 1))
    meet(beside, heads)
    size = QB_DEV // 2
    lanes = [(way, pair) for pair in range(pairs) for way in range(2)]

    def term_of(step, way, pair):
        owner = index_of(place - 1 - step if way == 0 else place + 1 + step)
        return terms[pair].at[pl.ds(owner * QB_DEV + way * size, size)]

    def fetch_of(step, way, pair):
        slot = step % 2
        return pltpu.make_async_copy(
            term_of(step, way, pair), own.at[way, pair, slot], own_sem.at[way, pair, slot]
        )

    swaps = []
    copies = {}
    fetches = {}
    for step in range(n):
        if step == 1:
            swaps = exchange(heads, sent_ref, got_ref.at[lax.axis_index("head")], *head_sems)
        for way, pair in lanes:
            if step > 0:
                copies[step - 1, way, pair].wait_recv()
                fetches[step, way, pair].wait()
                for b in range(size):
                    got = arrived[way, pair, step - 1, b].astype(jnp.float32)
                    got = (got + own[way, pair, step % 2, b].astype(jnp.float32)).astype(
                        jnp.bfloat16
                    )
                    if step < n - 1:
                        arrived[way, pair, step - 1, b] = got
                    else:
                        sums[pair][way * size + b] = got
            if step < n - 1:
                copies[step, way, pair] = pltpu.make_async_remote_copy(
                    src_ref=term_of(0, way, pair) if step == 0 else arrived.at[way, pair, step - 1],
                    dst_ref=arrived.at[way, pair, step],
                    send_sem=send_sem.at[way, pair, step],
                    recv_sem=recv_sem.at[way, pair, step],
                    device_id={"blk": beside[way]},
                    device_id_type=MESH,
                )
                copies[step, way, pair].start()
                fetches[step + 1, way, pair] = fetch_of(step + 1, way, pair)
                fetches[step + 1, way, pair].start()
    for copy in copies.values():
        copy.wait_send()
    for copy in swaps:
        copy.wait()


def reduce_blocks(sent, terms, n):
    pairs = len(terms)
    tail = terms[0].shape[1:]
    chunk = (QB_DEV // 2,) + tail
    steps = pltpu.SemaphoreType.DMA((2, pairs, n - 1))
    return pl.pallas_call(
        functools.partial(reduce_kernel, n, pairs, sent.shape[0]),
        out_shape=[jax.ShapeDtypeStruct(sent.shape, sent.dtype)]
        + [jax.ShapeDtypeStruct((QB_DEV,) + tail, jnp.bfloat16)] * pairs,
        in_specs=[pl.BlockSpec(memory_space=pl.ANY)] * (pairs + 1),
        out_specs=[pl.BlockSpec(memory_space=pl.ANY)]
        + [pl.BlockSpec(memory_space=pltpu.VMEM)] * pairs,
        scratch_shapes=[
            pltpu.VMEM((2, pairs, n - 1) + chunk, jnp.bfloat16),
            pltpu.VMEM((2, pairs, 2) + chunk, jnp.bfloat16),
            pltpu.SemaphoreType.DMA((2, pairs, 2)),
            steps,
            steps,
        ]
        + exchange_semaphores(sent.shape[0]),
        compiler_params=pltpu.CompilerParams(
            collective_id=1, has_side_effects=True, vmem_limit_bytes=(n + 12) << 20
        ),
    )(sent, *terms)


def on_device(
    query_rows,
    key_rows,
    value_rows,
    out_grad,
    expander_device,
    expander_block,
    local_offset,
    live_count,
    drop_seed,
):
    head_count = lax.axis_size("head")
    share_rows = query_rows.shape[0]
    local_width = query_rows.shape[1] // head_count
    pairs = local_width // PAIR
    peer_count = lax.axis_size("blk")
    blocks = peer_count * QB_DEV
    block_rows = QB_DEV * BS

    def for_heads(members):
        return jnp.stack(
            [m.reshape(share_rows, head_count, local_width).transpose(1, 0, 2) for m in members],
            axis=1,
        )

    def for_rows(members):
        return jnp.stack([m.reshape(head_count, share_rows, m.shape[-1]) for m in members], axis=1)

    def swapped(sent):
        return lax.all_to_all(sent, "head", split_axis=0, concat_axis=0, tiled=True)

    def as_blocks(got):
        return [got[:, n].reshape(block_rows, local_width) for n in range(got.shape[1])]

    def as_rows(got):
        return [got[:, n].transpose(1, 0, 2).reshape(share_rows, -1) for n in range(got.shape[1])]

    mine = lax.axis_index("blk") * QB_DEV + jnp.arange(QB_DEV, dtype=jnp.int32)[:, None]
    slots = jnp.concatenate(
        [mine, (mine + local_offset + blocks) % blocks, expander_device * QB_DEV + expander_block],
        axis=1,
    ).astype(jnp.int32)
    row = jnp.arange(BS, dtype=jnp.int32) * BS
    words = (drop_seed * 40503)[..., None] + row

    mixed = jnp.stack(
        [m.reshape(share_rows, head_count, pairs, PAIR) for m in (key_rows, value_rows)], axis=3
    )
    mixed = mixed.transpose(1, 0, 2, 3, 4).reshape(
        head_count, share_rows // BS, BS, pairs * 2 * PAIR
    )
    kv, got = gather_blocks(mixed, for_heads([query_rows, out_grad]), peer_count)
    query_local, grad_local = as_blocks(got)
    parts, terms = [], []
    for pair in range(pairs):
        pair_words = jnp.concatenate([words[2 * pair], words[2 * pair + 1]], axis=-1)
        att, dq, grads = attend(slots, live_count, query_local, grad_local, kv, pair_words, pair)
        parts.append((att, dq))
        terms.append(grads)
    row_results = [jnp.concatenate([part[n] for part in parts], axis=1) for n in range(2)]
    got, *sums = reduce_blocks(for_rows(row_results), terms, peer_count)
    sums = [m.reshape(block_rows, 2 * PAIR) for m in sums]
    grads = [
        jnp.concatenate([m[:, :PAIR] for m in sums], axis=1),
        jnp.concatenate([m[:, PAIR:] for m in sums], axis=1),
    ]
    return tuple(as_rows(got) + as_rows(swapped(for_rows(grads))))


def solution(mesh):
    rows = P(("blk", "head"), None)
    in_specs = (
        rows,
        rows,
        rows,
        rows,
        P("blk", None),
        P("blk", None),
        P("blk", None),
        P("blk"),
        P("head", "blk", None),
    )
    return jax.shard_map(
        on_device, mesh=mesh, in_specs=in_specs, out_specs=(rows,) * 4, check_vma=False
    )
```
